32 devices in a mesh: groups: 2 (over y), tensor: 16 (over z, x, core).
Axes of the slice: x: 2, y: 2, z: 4, core: 2. Of those that a mesh axis runs over, the one named last changes fastest.
Arguments:
- token_ids: int32 [16, 4], P('tensor', 'groups'), parts along dimension 1, may hold values from 0 to 63
- lengths: int32 [4], P('groups'), parts along dimension 0, may hold values from 8 to 16, as said below
- embed_table: bfloat16 [64, 6144], replicated, may hold values from -6 to 6
- gain_attn: float32 [6144], replicated, may hold values from 0.1 to 1.9
- w_qkv: bfloat16 [6144, 18432], P(None, 'tensor'), may hold values from -0.078125 to 0.078125
- w_out: bfloat16 [6144, 6144], P(None, 'tensor'), may hold values from -0.078125 to 0.078125
- gain_first: float32 [6144], replicated, may hold values from 0.1 to 1.9
- gate_first: bfloat16 [6144, 16384], P(None, 'tensor'), may hold values from -0.078125 to 0.078125
- up_first: bfloat16 [6144, 16384], P(None, 'tensor'), may hold values from -0.078125 to 0.078125
- down_first: bfloat16 [16384, 6144], P('tensor'), may hold values from -0.09375 to 0.09375
- gain_second: float32 [6144], replicated, may hold values from 0.1 to 1.9
- gate_second: bfloat16 [6144, 16384], P(None, 'tensor'), may hold values from -0.078125 to 0.078125
- up_second: bfloat16 [6144, 16384], P(None, 'tensor'), may hold values from -0.078125 to 0.078125
- down_second: bfloat16 [16384, 6144], P('tensor'), may hold values from -0.09375 to 0.09375
Outputs:
- states: bfloat16 [16, 4, 6144], P('tensor', 'groups'), parts along dimension 1
The draws below stay inside these ranges and needn't reach their ends.
There are 2 independent parts, one for each index of `groups`. The reference program is written for one: setup_inputs(seed, part) draws one part's arguments, and reference() takes and returns one part's arrays. A program takes and returns all parts, laid end to end along the dimension named above; an argument that names none is the same for every part. Nothing has to cross between parts.
Inputs may be any that keep to these rules, and one draw needn't show every extreme that they name: `lengths`: each micro-batch holds one protein of at least half of 16 positions; in every draw one micro-batch is full, 16 positions.
All inputs are finite; a program needn't handle non-finite values.
Results may differ from the reference program's by a relative error of at most 0.013.
Values may be sent and summed in bfloat16 or wider, within the bound.
A program may use at most 192 MiB of HBM per device.

```python
import jax
import jax.numpy as jnp
from jax import lax

D = 6144
H = 48
HD = 128
VOCAB = 64
FFW = 16384
MICRO = 2
MB_TOK = 16


def draw_lengths(key, part):
    first_key, second_key = jax.random.split(jax.random.fold_in(key, 17))
    base_len = jax.random.randint(first_key, (MICRO,), MB_TOK // 2, MB_TOK + 1)
    full_index = jax.random.randint(second_key, (), 0, MICRO)
    return jnp.where(jnp.arange(MICRO) == full_index, MB_TOK, base_len).astype(jnp.int32)


def place_ends(result, rng, least, top_value):
    index_at = [jax.random.randint(jax.random.fold_in(rng, axis), (), 0, length) for axis, length in enumerate(result.shape)]
    widest = result.shape.index(max(result.shape))
    beside = index_at[:widest] + [(index_at[widest] + 1) % result.shape[widest]] + index_at[widest + 1:]
    return result.at[tuple(index_at)].set(least).at[tuple(beside)].set(top_value)


def block_scale(rng, extent, cuts, low, high):
    factor_of = 1.0
    for axis_at, shards_of in cuts:
        heights = jax.random.uniform(jax.random.fold_in(jax.random.fold_in(rng, 6), axis_at), (shards_of,), jnp.float32, low / len(cuts), high / len(cuts))
        factor_of = factor_of * jnp.repeat(jnp.exp(heights), extent[axis_at] // shards_of).reshape((-1,) + (1,) * (len(extent) - 1 - axis_at))
    return factor_of


def gaussian(key, dims, width, most, cuts=(), dtype=jnp.bfloat16):
    entries = jax.random.normal(key, dims, jnp.float32) * width
    if len(cuts) > 0:
        entries = block_scale(key, dims, cuts, -0.22, 0.18) * entries
    return jnp.clip(entries, min=-most, max=most).astype(dtype)


def setup_inputs(seed: int = 0, part: int = 0) -> dict:
    seeds = jax.random.split(jax.random.key(seed), 15)
    part_keys = jax.random.split(jax.random.fold_in(seeds[14], part), 15)
    return {
        "token_ids": place_ends(jax.random.randint(part_keys[0], (MB_TOK, MICRO), 0, VOCAB), jax.random.fold_in(part_keys[0], 1), 0, VOCAB - 1).astype(jnp.int32),
        "lengths": draw_lengths(jax.random.fold_in(jax.random.fold_in(seeds[14], part), 71), part),
        "embed_table": gaussian(seeds[2], (VOCAB, D), 1.0, 6.0),
        "gain_attn": jnp.clip(1.0 + 0.18 * jax.random.normal(seeds[3], (D,), jnp.float32), 0.1, 1.9),
        "w_qkv": gaussian(seeds[4], (D, 3 * D), D ** -0.5, 0.078125, ((1, 16),)),
        "w_out": gaussian(seeds[5], (D, D), D ** -0.5, 0.078125, ((1, 16),)),
        "gain_first": jnp.clip(1.0 + 0.18 * jax.random.normal(seeds[6], (D,), jnp.float32), 0.1, 1.9),
        "gate_first": gaussian(seeds[7], (D, FFW), D ** -0.5, 0.078125, ((1, 16),)),
        "up_first": gaussian(seeds[8], (D, FFW), D ** -0.5, 0.078125, ((1, 16),)),
        "down_first": gaussian(seeds[9], (FFW, D), (FFW // 4) ** -0.5, 0.09375, ((0, 16),)),
        "gain_second": jnp.clip(1.0 + 0.18 * jax.random.normal(seeds[10], (D,), jnp.float32), 0.1, 1.9),
        "gate_second": gaussian(seeds[11], (D, FFW), D ** -0.5, 0.078125, ((1, 16),)),
        "up_second": gaussian(seeds[12], (D, FFW), D ** -0.5, 0.078125, ((1, 16),)),
        "down_second": gaussian(seeds[13], (FFW, D), (FFW // 4) ** -0.5, 0.09375, ((0, 16),)),
    }


def norm_rows(values, gain_vec):
    row_mean = lax.optimization_barrier(jnp.mean(values, axis=-1, keepdims=True))
    centred = values - row_mean
    row_var = lax.optimization_barrier(jnp.mean(centred * centred, axis=-1, keepdims=True))
    return (centred * lax.rsqrt(row_var + 1e-05) * gain_vec).astype(jnp.bfloat16)

def project(inputs, weight_mat):
    return jnp.einsum('pmd,dc->pmc', inputs.astype(jnp.float32), weight_mat.astype(jnp.float32))

def feed_forward(resid, gain_vec, gate_mat, up_mat, down_mat):
    normed = norm_rows(resid, gain_vec)
    hidden = (jax.nn.silu(project(normed, gate_mat)) * project(normed, up_mat)).astype(jnp.bfloat16)
    return resid + project(hidden, down_mat)

def reference(token_ids, lengths, embed_table, gain_attn, w_qkv, w_out, gain_first, gate_first, up_first, down_first, gain_second, gate_second, up_second, down_second):
    embedded = embed_table[token_ids].astype(jnp.float32)
    normed_attn = norm_rows(embedded, gain_attn)
    projected = project(normed_attn, w_qkv).astype(jnp.bfloat16)
    queries = projected[..., :D].reshape(MB_TOK, MICRO, H, HD).astype(jnp.float32)
    key_rows = projected[..., D:2 * D].reshape(MB_TOK, MICRO, H, HD).astype(jnp.float32)
    value_rows = projected[..., 2 * D:].reshape(MB_TOK, MICRO, H, HD).astype(jnp.float32)
    scores = jnp.einsum('pmhe,qmhe->pmhq', queries, key_rows) * HD ** (-0.5)
    live_keys = (jnp.arange(MB_TOK)[None, :] < lengths[:, None]).astype(jnp.float32)
    weights = jnp.exp(scores) * live_keys[None, :, None, :]
    denominator = lax.optimization_barrier(jnp.sum(weights, axis=-1))
    numerator = jnp.einsum('pmhq,qmhe->pmhe', weights.astype(jnp.bfloat16).astype(jnp.float32), value_rows)
    attended = (numerator / denominator[..., None]).reshape(MB_TOK, MICRO, D).astype(jnp.bfloat16)
    attn_proj = project(attended, w_out).astype(jnp.bfloat16)
    after_attn = embedded + attn_proj.astype(jnp.float32)
    after_first = feed_forward(after_attn, gain_first, gate_first, up_first, down_first)
    after_second = feed_forward(after_first, gain_second, gate_second, up_second, down_second)
    return after_second.astype(jnp.bfloat16)
```

```python
import functools

import jax
import jax.numpy as jnp
from jax import lax
from jax.experimental import pallas as pl
from jax.experimental.pallas import tpu as pltpu
from jax.sharding import PartitionSpec as P

HD = 128
LANES = 128
MESH = pl.DeviceIdType.MESH
F32 = jnp.float32
BF16 = jnp.bfloat16


def norm_rows(values, gain_vec):
    row_mean = jnp.mean(values, axis=-1, keepdims=True)
    centred = values - row_mean
    row_var = jnp.mean(centred * centred, axis=-1, keepdims=True)
    return (centred * lax.rsqrt(row_var + 1e-05) * gain_vec).astype(jnp.bfloat16)


def local_hidden(normed, gate_mat, up_mat):
    gated = jnp.einsum("pmd,dc->pmc", normed, gate_mat, preferred_element_type=jnp.float32)
    lifted = jnp.einsum("pmd,dc->pmc", normed, up_mat, preferred_element_type=jnp.float32)
    return (jax.nn.silu(gated) * lifted).astype(jnp.bfloat16)


def spread_rows(local_rows, row_fn):
    return row_fn(lax.all_gather(local_rows, "tensor", axis=0, tiled=True))


def to_tokens(columns):
    return lax.all_to_all(columns, "tensor", split_axis=0, concat_axis=2, tiled=True)


def local_general(
    token_ids, lengths, embed_table, gain_attn, w_qkv, w_out,
    gain_first, gate_first, up_first, down_first,
    gain_second, gate_second, up_second, down_second,
):
    rows_here, micro_count = token_ids.shape
    vocab_size, width = embed_table.shape
    heads = width // HD
    own_start = lax.axis_index("tensor") * rows_here
    onehot = (token_ids[:, :, None] == jnp.arange(vocab_size)[None, None, :]).astype(jnp.bfloat16)
    embedded = jnp.einsum("pmv,vd->pmd", onehot, embed_table, preferred_element_type=jnp.float32)

    def matmul_rows(weight):
        return lambda rows: jnp.einsum(
            "pmd,dc->pmc", rows, weight, preferred_element_type=jnp.float32
        ).astype(jnp.bfloat16)

    projected = to_tokens(spread_rows(norm_rows(embedded, gain_attn), matmul_rows(w_qkv)))
    queries = projected[..., :width].reshape(rows_here, micro_count, heads, HD)
    keys = lax.all_gather(projected[..., width : 2 * width], "tensor", axis=0, tiled=True)
    values = lax.all_gather(projected[..., 2 * width :], "tensor", axis=0, tiled=True)
    total = keys.shape[0]
    keys = keys.reshape(total, micro_count, heads, HD)
    values = values.reshape(total, micro_count, heads, HD)
    scores = jnp.einsum("pmhe,qmhe->pmhq", queries, keys, preferred_element_type=jnp.float32)
    live = (jnp.arange(total)[None, :] < lengths[:, None]).astype(jnp.float32)
    weights = jnp.exp(scores * HD ** (-0.5)) * live[None, :, None, :]
    numerator = jnp.einsum(
        "pmhq,qmhe->pmhe", weights.astype(jnp.bfloat16), values, preferred_element_type=jnp.float32
    )
    attended = numerator / jnp.sum(weights, axis=-1)[..., None]
    attended = attended.reshape(rows_here, micro_count, width).astype(jnp.bfloat16)
    after_attn = embedded + to_tokens(spread_rows(attended, matmul_rows(w_out))).astype(jnp.float32)
    hidden_first = spread_rows(
        norm_rows(after_attn, gain_first), lambda rows: local_hidden(rows, gate_first, up_first)
    )
    partial_all = jnp.einsum(
        "pmc,cd->pmd", hidden_first, down_first, preferred_element_type=jnp.float32
    )
    own_rows = lax.dynamic_slice_in_dim(partial_all, own_start, rows_here, 0) + after_attn
    partial_all = lax.dynamic_update_slice_in_dim(partial_all, own_rows, own_start, 0)
    first_all = lax.psum(partial_all, "tensor")
    after_first = lax.dynamic_slice_in_dim(first_all, own_start, rows_here, 0)
    hidden_second = local_hidden(norm_rows(first_all, gain_second), gate_second, up_second)
    second = jnp.einsum(
        "pmc,cd->pmd", hidden_second, down_second, preferred_element_type=jnp.float32
    )
    after_second = after_first + lax.psum_scatter(
        second, "tensor", scatter_dimension=0, tiled=True
    )
    return after_second.astype(jnp.bfloat16)


def fused_kernel(
    n, micro, vocab, kc,
    tok_ref, len_ref, emb_hbm, ga_hbm, wq_hbm, wo_hbm,
    gf_hbm, g1_hbm, u1_hbm, d1_hbm, gs_hbm, g2_hbm, u2_hbm, d2_hbm,
    out_ref,
    buf_a, buf_o, buf_g, buf_u, buf_d,
    emb_ref, gain_ref,
    toks, onehot, resid, normed, blocks, qkv, full, acc, cout, crecv, xout, xrecv, zout, zrecv,
    own, fin, finr, rows_out,
    w_sem, e_sem, small_send, small_recv, q_send, q_recv, ag_send, ag_recv,
    rs_send, rs_recv, f_send, f_recv,
):
    width = emb_ref.shape[1]
    pos = n
    rows = micro * pos
    shard = width // n
    hidden_cols = buf_g.shape[1]
    hpd = width // HD // n
    nblk = 3 * hpd
    heads = width // HD
    nz = n // 4
    chunks = width // kc
    sub = shard // LANES

    me = lax.axis_index("tensor")
    grp = lax.axis_index("groups")
    core = lax.rem(me, 2)
    xbit = lax.rem(me // 2, 2)
    zpos = me // 4
    cpeer = me + 1 - 2 * core
    xpeer = me + 2 - 4 * xbit

    def zmove(dev, k):
        return lax.rem(dev + 4 * k + n, n)

    def rcopy(src, dst, ssem, rsem, dev):
        return pltpu.make_async_remote_copy(
            src_ref=src, dst_ref=dst, send_sem=ssem, recv_sem=rsem,
            device_id=(grp, dev), device_id_type=MESH,
        )

    def row_chunk(ref, c):
        return ref.at[pl.ds(c * kc, kc)]

    dk = hidden_cols // 4

    def w_copies(which):
        if which == "q":
            return [pltpu.make_async_copy(row_chunk(wq_hbm, c), row_chunk(buf_a, c), w_sem.at[0, c]) for c in range(chunks)]
        if which == "o":
            return [pltpu.make_async_copy(row_chunk(wo_hbm, c), row_chunk(buf_o, c), w_sem.at[1, c]) for c in range(chunks)]
        if which == "g1":
            return [pltpu.make_async_copy(row_chunk(g1_hbm, c), row_chunk(buf_g, c), w_sem.at[2, c]) for c in range(chunks)]
        if which == "u1":
            return [pltpu.make_async_copy(row_chunk(u1_hbm, c), row_chunk(buf_u, c), w_sem.at[3, c]) for c in range(chunks)]
        if which == "g2":
            return [
                pltpu.make_async_copy(
                    row_chunk(g2_hbm, c), buf_a.at[pl.ds(c * kc, kc), pl.ds(0, hidden_cols)], w_sem.at[4, c]
                )
                for c in range(chunks)
            ]
        if which == "u2":
            return [pltpu.make_async_copy(row_chunk(u2_hbm, c), row_chunk(buf_g, c), w_sem.at[5, c]) for c in range(chunks)]
        src = d1_hbm if which == "d1" else d2_hbm
        row = 6 if which == "d1" else 7
        return [
            pltpu.make_async_copy(src.at[pl.ds(c * dk, dk)], buf_d.at[pl.ds(c * dk, dk)], w_sem.at[row, c])
            for c in range(4)
        ]

    def start_all(which):
        for cp in w_copies(which):
            cp.start()

    def wait_all(which):
        for cp in w_copies(which):
            cp.wait()

    small = [
        pltpu.make_async_copy(emb_hbm, emb_ref, e_sem.at[0]),
        pltpu.make_async_copy(ga_hbm, gain_ref.at[0], e_sem.at[1]),
        pltpu.make_async_copy(gf_hbm, gain_ref.at[1], e_sem.at[2]),
        pltpu.make_async_copy(gs_hbm, gain_ref.at[2], e_sem.at[3]),
    ]
    for cp in small:
        cp.start()
    start_all("q")
    start_all("o")
    start_all("g1")

    tile_row = lax.broadcasted_iota(jnp.int32, (8, LANES), 0)
    tile = jnp.zeros((8, LANES), jnp.int32)
    for m in range(micro):
        tile = jnp.where(tile_row == m, tok_ref[0, m], tile)
    toks[me] = tile

    barrier = pltpu.get_barrier_semaphore()
    for k in range(1, n):
        pl.semaphore_signal(barrier, inc=1, device_id=(grp, lax.rem(me + k, n)), device_id_type=MESH)
    pl.semaphore_wait(barrier, n - 1)

    tok_sends = [
        rcopy(toks.at[me], toks.at[me], small_send.at[k], small_recv.at[k], lax.rem(me + k, n))
        for k in range(1, n)
    ]
    for cp in tok_sends:
        cp.start()
    for k in range(1, n):
        src = lax.rem(me + n - k, n)
        rcopy(toks.at[src], toks.at[src], small_send.at[k], small_recv.at[k], src).wait_recv()

    lane = lax.broadcasted_iota(jnp.int32, (1, vocab), 1)
    for p in range(pos):
        for m in range(micro):
            onehot[m * pos + p : m * pos + p + 1, :] = (toks[p, m : m + 1, :vocab] == lane).astype(F32)
    for cp in small:
        cp.wait()
    hot = onehot[...].astype(BF16)
    for c in range(chunks):
        sl = slice(c * kc, (c + 1) * kc)
        resid[:, sl] = jnp.dot(hot, emb_ref[:, sl], preferred_element_type=F32)

    def norm_into(index):
        total = jnp.zeros((rows, 1), F32)
        for c in range(chunks):
            total += jnp.sum(resid[:, c * kc : (c + 1) * kc], axis=1, keepdims=True)
        mean = total * (1.0 / width)
        var = jnp.zeros((rows, 1), F32)
        for c in range(chunks):
            cen = resid[:, c * kc : (c + 1) * kc] - mean
            var += jnp.sum(cen * cen, axis=1, keepdims=True)
        inv = lax.rsqrt(var * (1.0 / width) + 1e-05)
        for c in range(chunks):
            sl = slice(c * kc, (c + 1) * kc)
            normed[:, sl] = ((resid[:, sl] - mean) * inv * gain_ref[index, :, sl]).astype(BF16)

    norm_into(0)

    part = jnp.zeros((rows, nblk * HD), F32)
    q_copies = w_copies("q")
    for c in range(chunks):
        q_copies[c].wait()
        part += jnp.dot(
            normed[:, c * kc : (c + 1) * kc], buf_a[c * kc : (c + 1) * kc, :], preferred_element_type=F32
        )
    for j in range(nblk):
        blocks[j] = part[:, j * HD : (j + 1) * HD].astype(BF16)

    def block_target(j):
        g = me * nblk + j
        kind = g // heads
        head = lax.rem(g, heads)
        return head // hpd, kind * hpd + lax.rem(head, hpd)

    for j in range(nblk):
        owner, slot = block_target(j)

        @pl.when(owner != me)
        def _():
            rcopy(blocks.at[j], qkv.at[slot], q_send.at[j], q_recv.at[slot], owner).start()

        @pl.when(owner == me)
        def _():
            pltpu.make_async_copy(blocks.at[j], qkv.at[slot], q_recv.at[slot]).start()

    start_all("u1")
    start_all("d1")
    start_all("g2")

    for slot in range(nblk):
        pltpu.make_async_copy(blocks.at[0], qkv.at[slot], q_recv.at[slot]).wait()

    ri = lax.broadcasted_iota(jnp.int32, (rows, rows), 0)
    ci = lax.broadcasted_iota(jnp.int32, (rows, rows), 1)
    live = jnp.zeros((rows, rows), F32)
    for m in range(micro):
        inside = (ri >= m * pos) & (ri < (m + 1) * pos) & (ci >= m * pos) & (ci < m * pos + len_ref[m])
        live = jnp.where(inside, 1.0, live)
    for h in range(hpd):
        scores = lax.dot_general(
            qkv[h], qkv[hpd + h], (((1,), (1,)), ((), ())), preferred_element_type=F32
        ) * (HD ** (-0.5))
        weights = jnp.where(live > 0.5, jnp.exp(scores), 0.0)
        denominator = jnp.sum(weights, axis=1, keepdims=True)
        numerator = jnp.dot(weights.astype(BF16), qkv[2 * hpd + h], preferred_element_type=F32)
        full[0, me, :, h * HD : (h + 1) * HD] = (numerator / denominator).astype(BF16)

    def gather(ph):
        buf = full.at[ph]
        sends = []

        def send(slot, idx, dev):
            cp = rcopy(buf.at[slot], buf.at[slot], ag_send.at[ph, idx], ag_recv.at[ph, idx], dev)
            cp.start()
            sends.append(cp)

        def arrive(slot, idx):
            rcopy(buf.at[slot], buf.at[slot], ag_send.at[ph, idx], ag_recv.at[ph, idx], cpeer).wait_recv()

        xbase, cbase = nz, 2 * nz
        for k in range(1, nz):
            send(me, k, zmove(me, k))
        send(me, xbase, xpeer)
        send(me, cbase, cpeer)
        for k in range(1, nz):
            src = zmove(me, -k)
            arrive(src, k)
            send(src, xbase + k, xpeer)
            send(src, cbase + k, cpeer)
        for k in range(nz):
            src = zmove(xpeer, -k)
            arrive(src, xbase + k)
            send(src, cbase + nz + k, cpeer)
        xc = cpeer + 2 - 4 * xbit
        for k in range(nz):
            arrive(zmove(cpeer, -k), cbase + k)
            arrive(zmove(xc, -k), cbase + nz + k)
        return sends

    sends0 = gather(0)
    for s in range(n):
        normed[:, s * shard : (s + 1) * shard] = full[0, s]

    part = jnp.zeros((rows, shard), F32)
    o_copies = w_copies("o")
    for c in range(chunks):
        o_copies[c].wait()
        part += jnp.dot(
            normed[:, c * kc : (c + 1) * kc], buf_o[c * kc : (c + 1) * kc, :], preferred_element_type=F32
        )
    full[1, me] = part.astype(BF16)
    sends1 = gather(1)
    for s in range(n):
        sl = slice(s * shard, (s + 1) * shard)
        resid[:, sl] = resid[:, sl] + full[1, s].astype(F32)

    def feed(gate_buf, up_buf, names, index):
        norm_into(index)
        g_copies, u_copies = w_copies(names[0]), w_copies(names[1])
        gated = jnp.zeros((rows, hidden_cols), F32)
        lifted = jnp.zeros((rows, hidden_cols), F32)
        for c in range(chunks):
            x = normed[:, c * kc : (c + 1) * kc]
            g_copies[c].wait()
            gated += jnp.dot(x, gate_buf[c * kc : (c + 1) * kc, :hidden_cols], preferred_element_type=F32)
        for c in range(chunks):
            x = normed[:, c * kc : (c + 1) * kc]
            u_copies[c].wait()
            lifted += jnp.dot(x, up_buf[c * kc : (c + 1) * kc, :], preferred_element_type=F32)
        return (gated / (1.0 + jnp.exp(-gated)) * lifted).astype(BF16)

    def down_reduce(hidden, ph):
        sends = []
        for j in range(2 * nz):
            k = j % nz
            xsel = (1 - xbit) if j < nz else xbit
            q = lax.rem(zpos + k, nz) * 2 + xsel
            both = jnp.dot(
                hidden,
                buf_d[:, pl.ds(pl.multiple_of(q * 2 * shard, LANES), 2 * shard)],
                preferred_element_type=F32,
            )
            left, right = both[:, :shard], both[:, shard:]
            is_left = jnp.zeros((rows, shard), jnp.int32) + core == 0
            acc[j] = jnp.where(is_left, left, right)
            cout[ph, j] = jnp.where(is_left, right, left).astype(BF16)
            cp = rcopy(cout.at[ph, j], crecv.at[ph, j], rs_send.at[ph, j], rs_recv.at[ph, j], cpeer)
            cp.start()
            sends.append(cp)
        for k in range(nz):
            sends[k].wait_recv()
            xout[ph, k] = (acc[k] + crecv[ph, k].astype(F32)).astype(BF16)
            cp = rcopy(
                xout.at[ph, k], xrecv.at[ph, k],
                rs_send.at[ph, 2 * nz + k], rs_recv.at[ph, 2 * nz + k], xpeer,
            )
            cp.start()
            sends.append(cp)
        for k in list(range(1, nz)) + [0]:
            sends[nz + k].wait_recv()
            sends[2 * nz + k].wait_recv()
            val = acc[nz + k] + crecv[ph, nz + k].astype(F32) + xrecv[ph, k].astype(F32)
            if k:
                zout[ph, k] = val.astype(BF16)
                cp = rcopy(
                    zout.at[ph, k], zrecv.at[ph, k],
                    rs_send.at[ph, 3 * nz + k], rs_recv.at[ph, 3 * nz + k], zmove(me, k),
                )
                cp.start()
                sends.append(cp)
            else:
                own[...] = val
        for k in range(1, nz):
            sends[3 * nz + k - 1].wait_recv()
            own[...] = own[...] + zrecv[ph, k].astype(F32)
        return sends

    hidden = feed(buf_g, buf_u, ("g1", "u1"), 1)
    start_all("u2")
    wait_all("d1")
    sends2 = down_reduce(hidden, 0)
    start_all("d2")
    full[2, me] = own[...].astype(BF16)
    sends3 = gather(2)
    for s in range(n):
        sl = slice(s * shard, (s + 1) * shard)
        resid[:, sl] = resid[:, sl] + full[2, s].astype(F32)

    hidden = feed(buf_a, buf_g, ("g2", "u2"), 2)
    wait_all("d2")
    sends4 = down_reduce(hidden, 1)
    own[...] = own[...] + resid[:, pl.ds(pl.multiple_of(me * shard, LANES), shard)]

    for p in range(pos):
        for m in range(micro):
            for k in range(sub):
                fin[p, m * sub + k : m * sub + k + 1, :] = own[m * pos + p : m * pos + p + 1, k * LANES : (k + 1) * LANES]
    fin_sends = []
    for k in range(1, n):
        dev = lax.rem(me + k, n)
        cp = rcopy(fin.at[dev], finr.at[me], f_send.at[k], f_recv.at[k], dev)
        cp.start()
        fin_sends.append(cp)
    finr[me] = fin[me]
    for k in range(1, n):
        src = lax.rem(me + n - k, n)
        rcopy(fin.at[src], finr.at[src], f_send.at[k], f_recv.at[k], src).wait_recv()
    for s in range(n):
        for m in range(micro):
            for k in range(sub):
                lo = s * shard + k * LANES
                rows_out[m : m + 1, lo : lo + LANES] = finr[s, m * sub + k : m * sub + k + 1, :]
    out_ref[0] = rows_out[...].astype(BF16)

    for cp in tok_sends + sends0 + sends1 + sends2 + sends3 + sends4 + fin_sends:
        cp.wait_send()
    for j in range(nblk):
        owner, slot = block_target(j)

        @pl.when(owner != me)
        def _():
            rcopy(blocks.at[j], qkv.at[slot], q_send.at[j], q_recv.at[slot], owner).wait_send()


def local_fused(n, kc, *args):
    token_ids, lengths, embed_table = args[:3]
    micro = token_ids.shape[1]
    vocab, width = embed_table.shape
    rows = n * micro
    shard = width // n
    hidden_cols = args[7].shape[1]
    nblk = 3 * width // HD // n
    nz = n // 4
    chunks = width // kc
    tall = lambda gain: gain.reshape(1, width)
    operands = list(args)
    for at in (3, 6, 10):
        operands[at] = tall(args[at])
    smem = pl.BlockSpec(memory_space=pltpu.SMEM)
    hbm = pl.BlockSpec(memory_space=pl.ANY)
    dma = pltpu.SemaphoreType.DMA
    weight_bytes = sum(a.size * a.dtype.itemsize for a in args)
    return pl.pallas_call(
        functools.partial(fused_kernel, n, micro, vocab, kc),
        out_shape=jax.ShapeDtypeStruct((1, micro, width), BF16),
        in_specs=[smem, smem] + [hbm] * 12,
        out_specs=pl.BlockSpec(memory_space=pltpu.VMEM),
        scratch_shapes=[
            pltpu.VMEM((width, nblk * HD), BF16),
            pltpu.VMEM((width, shard), BF16),
            pltpu.VMEM((width, hidden_cols), BF16),
            pltpu.VMEM((width, hidden_cols), BF16),
            pltpu.VMEM((hidden_cols, width), BF16),
            pltpu.VMEM((vocab, width), BF16),
            pltpu.VMEM((3, 1, width), F32),
            pltpu.VMEM((n, 8, LANES), jnp.int32),
            pltpu.VMEM((rows, vocab), F32),
            pltpu.VMEM((rows, width), F32),
            pltpu.VMEM((rows, width), BF16),
            pltpu.VMEM((nblk, rows, HD), BF16),
            pltpu.VMEM((nblk, rows, HD), BF16),
            pltpu.VMEM((3, n, rows, shard), BF16),
            pltpu.VMEM((2 * nz, rows, shard), F32),
            pltpu.VMEM((2, 2 * nz, rows, shard), BF16),
            pltpu.VMEM((2, 2 * nz, rows, shard), BF16),
            pltpu.VMEM((2, nz, rows, shard), BF16),
            pltpu.VMEM((2, nz, rows, shard), BF16),
            pltpu.VMEM((2, nz, rows, shard), BF16),
            pltpu.VMEM((2, nz, rows, shard), BF16),
            pltpu.VMEM((rows, shard), F32),
            pltpu.VMEM((n, 8, LANES), F32),
            pltpu.VMEM((n, 8, LANES), F32),
            pltpu.VMEM((micro, width), F32),
            dma((8, max(chunks, 4))),
            dma((4,)),
            dma((n,)),
            dma((n,)),
            dma((nblk,)),
            dma((nblk,)),
            dma((3, n)),
            dma((3, n)),
            dma((2, n)),
            dma((2, n)),
            dma((n,)),
            dma((n,)),
        ],
        compiler_params=pltpu.CompilerParams(
            collective_id=0, has_side_effects=True, vmem_limit_bytes=63 * 1024 * 1024
        ),
        cost_estimate=pl.CostEstimate(
            flops=rows * weight_bytes, bytes_accessed=weight_bytes, transcendentals=0
        ),
    )(*operands)


def local(n, *args):
    token_ids, embed_table = args[0], args[2]
    width, hidden_cols = embed_table.shape[1], args[7].shape[1]
    rows_here, micro = token_ids.shape
    kc = next((k for k in (1024, 512, 256, LANES) if width % k == 0), 0)
    fits = (
        rows_here == 1
        and n % 4 == 0
        and kc > 0
        and width % (n * HD) == 0
        and hidden_cols % LANES == 0
        and hidden_cols <= args[4].shape[1]
        and micro * (width // n // LANES) <= 8
        and (micro * n) % 16 == 0
        and embed_table.shape[0] <= LANES
        and sum(a.size * a.dtype.itemsize for a in args) <= 100 * 1024 * 1024
    )
    return local_fused(n, kc, *args) if fits else local_general(*args)


def solution(mesh):
    return jax.shard_map(
        functools.partial(local, mesh.shape["tensor"]),
        mesh=mesh,
        in_specs=(
            P("tensor", "groups"),
            P("groups"),
            P(),
            P(),
            P(None, "tensor"),
            P(None, "tensor"),
            P(),
            P(None, "tensor"),
            P(None, "tensor"),
            P("tensor", None),
            P(),
            P(None, "tensor"),
            P(None, "tensor"),
            P("tensor", None),
        ),
        out_specs=P("tensor", "groups", None),
        check_vma=False,
    )
```

```python
import functools

import jax
import jax.numpy as jnp
from jax import lax
from jax.experimental import pallas as pl
from jax.experimental.pallas import tpu as pltpu
from jax.sharding import PartitionSpec as P

HD = 128
LANES = 128
MESH = pl.DeviceIdType.MESH
F32 = jnp.float32
BF16 = jnp.bfloat16


def norm_rows(values, gain_vec):
    row_mean = jnp.mean(values, axis=-1, keepdims=True)
    centred = values - row_mean
    row_var = jnp.mean(centred * centred, axis=-1, keepdims=True)
    return (centred * lax.rsqrt(row_var + 1e-05) * gain_vec).astype(jnp.bfloat16)


def local_hidden(normed, gate_mat, up_mat):
    gated = jnp.einsum("pmd,dc->pmc", normed, gate_mat, preferred_element_type=jnp.float32)
    lifted = jnp.einsum("pmd,dc->pmc", normed, up_mat, preferred_element_type=jnp.float32)
    return (jax.nn.silu(gated) * lifted).astype(jnp.bfloat16)


def spread_rows(local_rows, row_fn):
    return row_fn(lax.all_gather(local_rows, "tensor", axis=0, tiled=True))


def to_tokens(columns):
    return lax.all_to_all(columns, "tensor", split_axis=0, concat_axis=2, tiled=True)


def local_general(
    token_ids, lengths, embed_table, gain_attn, w_qkv, w_out,
    gain_first, gate_first, up_first, down_first,
    gain_second, gate_second, up_second, down_second,
):
    rows_here, micro_count = token_ids.shape
    vocab_size, width = embed_table.shape
    heads = width // HD
    own_start = lax.axis_index("tensor") * rows_here
    onehot = (token_ids[:, :, None] == jnp.arange(vocab_size)[None, None, :]).astype(jnp.bfloat16)
    embedded = jnp.einsum("pmv,vd->pmd", onehot, embed_table, preferred_element_type=jnp.float32)

    def matmul_rows(weight):
        return lambda rows: jnp.einsum(
            "pmd,dc->pmc", rows, weight, preferred_element_type=jnp.float32
        ).astype(jnp.bfloat16)

    projected = to_tokens(spread_rows(norm_rows(embedded, gain_attn), matmul_rows(w_qkv)))
    queries = projected[..., :width].reshape(rows_here, micro_count, heads, HD)
    keys = lax.all_gather(projected[..., width : 2 * width], "tensor", axis=0, tiled=True)
    values = lax.all_gather(projected[..., 2 * width :], "tensor", axis=0, tiled=True)
    total = keys.shape[0]
    keys = keys.reshape(total, micro_count, heads, HD)
    values = values.reshape(total, micro_count, heads, HD)
    scores = jnp.einsum("pmhe,qmhe->pmhq", queries, keys, preferred_element_type=jnp.float32)
    live = (jnp.arange(total)[None, :] < lengths[:, None]).astype(jnp.float32)
    weights = jnp.exp(scores * HD ** (-0.5)) * live[None, :, None, :]
    numerator = jnp.einsum(
        "pmhq,qmhe->pmhe", weights.astype(jnp.bfloat16), values, preferred_element_type=jnp.float32
    )
    attended = numerator / jnp.sum(weights, axis=-1)[..., None]
    attended = attended.reshape(rows_here, micro_count, width).astype(jnp.bfloat16)
    after_attn = embedded + to_tokens(spread_rows(attended, matmul_rows(w_out))).astype(jnp.float32)
    hidden_first = spread_rows(
        norm_rows(after_attn, gain_first), lambda rows: local_hidden(rows, gate_first, up_first)
    )
    partial_all = jnp.einsum(
        "pmc,cd->pmd", hidden_first, down_first, preferred_element_type=jnp.float32
    )
    own_rows = lax.dynamic_slice_in_dim(partial_all, own_start, rows_here, 0) + after_attn
    partial_all = lax.dynamic_update_slice_in_dim(partial_all, own_rows, own_start, 0)
    first_all = lax.psum(partial_all, "tensor")
    after_first = lax.dynamic_slice_in_dim(first_all, own_start, rows_here, 0)
    hidden_second = local_hidden(norm_rows(first_all, gain_second), gate_second, up_second)
    second = jnp.einsum(
        "pmc,cd->pmd", hidden_second, down_second, preferred_element_type=jnp.float32
    )
    after_second = after_first + lax.psum_scatter(
        second, "tensor", scatter_dimension=0, tiled=True
    )
    return after_second.astype(jnp.bfloat16)


def fused_kernel(
    n, micro, vocab, kc,
    tok_ref, len_ref, emb_hbm, ga_hbm, wq_hbm, wo_hbm,
    gf_hbm, g1_hbm, u1_hbm, d1_hbm, gs_hbm, g2_hbm, u2_hbm, d2_hbm,
    out_ref,
    buf_a, buf_o, buf_g, buf_u, buf_d,
    emb_ref, gain_ref,
    toks, onehot, resid, normed, blocks, qkv, full, acc, cout, crecv, xout, xrecv, zout, zrecv,
    own, fin, finr, rows_out,
    w_sem, e_sem, small_send, small_recv, q_send, q_recv, ag_send, ag_recv,
    rs_send, rs_recv, f_send, f_recv,
):
    width = emb_ref.shape[1]
    pos = n
    rows = micro * pos
    shard = width // n
    hidden_cols = buf_g.shape[1]
    hpd = width // HD // n
    nblk = 3 * hpd
    heads = width // HD
    nz = n // 4
    chunks = width // kc
    sub = shard // LANES

    me = lax.axis_index("tensor")
    grp = lax.axis_index("groups")
    core = lax.rem(me, 2)
    xbit = lax.rem(me // 2, 2)
    zpos = me // 4
    cpeer = me + 1 - 2 * core
    xpeer = me + 2 - 4 * xbit

    def zmove(dev, k):
        return lax.rem(dev + 4 * k + n, n)

    def rcopy(src, dst, ssem, rsem, dev):
        return pltpu.make_async_remote_copy(
            src_ref=src, dst_ref=dst, send_sem=ssem, recv_sem=rsem,
            device_id=(grp, dev), device_id_type=MESH,
        )

    def row_chunk(ref, c):
        return ref.at[pl.ds(c * kc, kc)]

    dparts = 8
    dk = hidden_cols // dparts

    def w_copies(which):
        if which == "q":
            return [pltpu.make_async_copy(row_chunk(wq_hbm, c), row_chunk(buf_a, c), w_sem.at[0, c]) for c in range(chunks)]
        if which == "o":
            return [pltpu.make_async_copy(row_chunk(wo_hbm, c), row_chunk(buf_o, c), w_sem.at[1, c]) for c in range(chunks)]
        if which == "g1":
            return [pltpu.make_async_copy(row_chunk(g1_hbm, c), row_chunk(buf_g, c), w_sem.at[2, c]) for c in range(chunks)]
        if which == "u1":
            return [pltpu.make_async_copy(row_chunk(u1_hbm, c), row_chunk(buf_u, c), w_sem.at[3, c]) for c in range(chunks)]
        if which == "g2":
            return [
                pltpu.make_async_copy(
                    row_chunk(g2_hbm, c), buf_a.at[pl.ds(c * kc, kc), pl.ds(0, hidden_cols)], w_sem.at[4, c]
                )
                for c in range(chunks)
            ]
        if which == "u2":
            return [pltpu.make_async_copy(row_chunk(u2_hbm, c), row_chunk(buf_g, c), w_sem.at[5, c]) for c in range(chunks)]
        src = d1_hbm if which == "d1" else d2_hbm
        row = 6 if which == "d1" else 7
        return [
            pltpu.make_async_copy(src.at[pl.ds(c * dk, dk)], buf_d.at[pl.ds(c * dk, dk)], w_sem.at[row, c])
            for c in range(dparts)
        ]

    pending = []

    def issue(count):
        for cp in pending[:count]:
            cp.start()
        del pending[:count]

    def wait_all(which):
        for cp in w_copies(which):
            cp.wait()

    small = [
        pltpu.make_async_copy(emb_hbm, emb_ref, e_sem.at[0]),
        pltpu.make_async_copy(ga_hbm, gain_ref.at[0], e_sem.at[1]),
        pltpu.make_async_copy(gf_hbm, gain_ref.at[1], e_sem.at[2]),
        pltpu.make_async_copy(gs_hbm, gain_ref.at[2], e_sem.at[3]),
    ]
    for cp in small:
        cp.start()
    pending.extend(w_copies("q") + w_copies("o") + w_copies("g1") + w_copies("u1") + w_copies("d1"))
    issue(chunks // 2)

    tile_row = lax.broadcasted_iota(jnp.int32, (8, LANES), 0)
    tile = jnp.zeros((8, LANES), jnp.int32)
    for m in range(micro):
        tile = jnp.where(tile_row == m, tok_ref[0, m], tile)
    toks[me] = tile

    barrier = pltpu.get_barrier_semaphore()
    for k in range(1, n):
        pl.semaphore_signal(barrier, inc=1, device_id=(grp, lax.rem(me + k, n)), device_id_type=MESH)
    pl.semaphore_wait(barrier, n - 1)

    tok_sends = [
        rcopy(toks.at[me], toks.at[me], small_send.at[k], small_recv.at[k], lax.rem(me + k, n))
        for k in range(1, n)
    ]
    for cp in tok_sends:
        cp.start()
    issue(chunks - chunks // 2)
    for k in range(1, n):
        src = lax.rem(me + n - k, n)
        rcopy(toks.at[src], toks.at[src], small_send.at[k], small_recv.at[k], src).wait_recv()

    lane = lax.broadcasted_iota(jnp.int32, (1, vocab), 1)
    for p in range(pos):
        for m in range(micro):
            onehot[m * pos + p : m * pos + p + 1, :] = (toks[p, m : m + 1, :vocab] == lane).astype(F32)
    for cp in small:
        cp.wait()
    hot = onehot[...].astype(BF16)
    for c in range(chunks):
        sl = slice(c * kc, (c + 1) * kc)
        resid[:, sl] = jnp.dot(hot, emb_ref[:, sl], preferred_element_type=F32)

    def norm_into(index):
        total = jnp.zeros((rows, 1), F32)
        for c in range(chunks):
            total += jnp.sum(resid[:, c * kc : (c + 1) * kc], axis=1, keepdims=True)
        mean = total * (1.0 / width)
        var = jnp.zeros((rows, 1), F32)
        for c in range(chunks):
            cen = resid[:, c * kc : (c + 1) * kc] - mean
            var += jnp.sum(cen * cen, axis=1, keepdims=True)
        inv = lax.rsqrt(var * (1.0 / width) + 1e-05)
        for c in range(chunks):
            sl = slice(c * kc, (c + 1) * kc)
            normed[:, sl] = ((resid[:, sl] - mean) * inv * gain_ref[index, :, sl]).astype(BF16)

    norm_into(0)

    part = jnp.zeros((rows, nblk * HD), F32)
    q_copies = w_copies("q")
    for c in range(chunks):
        q_copies[c].wait()
        part += jnp.dot(
            normed[:, c * kc : (c + 1) * kc], buf_a[c * kc : (c + 1) * kc, :], preferred_element_type=F32
        )
    for j in range(nblk):
        blocks[j] = part[:, j * HD : (j + 1) * HD].astype(BF16)

    def block_target(j):
        g = me * nblk + j
        kind = g // heads
        head = lax.rem(g, heads)
        return head // hpd, kind * hpd + lax.rem(head, hpd)

    for j in range(nblk):
        owner, slot = block_target(j)

        @pl.when(owner != me)
        def _():
            rcopy(blocks.at[j], qkv.at[slot], q_send.at[j], q_recv.at[slot], owner).start()

        @pl.when(owner == me)
        def _():
            pltpu.make_async_copy(blocks.at[j], qkv.at[slot], q_recv.at[slot]).start()

    pending.extend(w_copies("g2"))
    issue(chunks + 2 * chunks // 3)

    for slot in range(nblk):
        pltpu.make_async_copy(blocks.at[0], qkv.at[slot], q_recv.at[slot]).wait()

    ri = lax.broadcasted_iota(jnp.int32, (rows, rows), 0)
    ci = lax.broadcasted_iota(jnp.int32, (rows, rows), 1)
    live = jnp.zeros((rows, rows), F32)
    for m in range(micro):
        inside = (ri >= m * pos) & (ri < (m + 1) * pos) & (ci >= m * pos) & (ci < m * pos + len_ref[m])
        live = jnp.where(inside, 1.0, live)
    for h in range(hpd):
        scores = lax.dot_general(
            qkv[h], qkv[hpd + h], (((1,), (1,)), ((), ())), preferred_element_type=F32
        ) * (HD ** (-0.5))
        weights = jnp.where(live > 0.5, jnp.exp(scores), 0.0)
        denominator = jnp.sum(weights, axis=1, keepdims=True)
        numerator = jnp.dot(weights.astype(BF16), qkv[2 * hpd + h], preferred_element_type=F32)
        full[0, me, :, h * HD : (h + 1) * HD] = (numerator / denominator).astype(BF16)

    def gather(ph):
        buf = full.at[ph]
        sends = []

        def send(slot, idx, dev):
            cp = rcopy(buf.at[slot], buf.at[slot], ag_send.at[ph, idx], ag_recv.at[ph, idx], dev)
            cp.start()
            sends.append(cp)

        def arrive(slot, idx):
            rcopy(buf.at[slot], buf.at[slot], ag_send.at[ph, idx], ag_recv.at[ph, idx], cpeer).wait_recv()

        xbase, cbase = nz, 2 * nz
        for k in range(1, nz):
            send(me, k, zmove(me, k))
        send(me, xbase, xpeer)
        send(me, cbase, cpeer)
        issue(1)
        for k in range(1, nz):
            src = zmove(me, -k)
            arrive(src, k)
            send(src, xbase + k, xpeer)
            send(src, cbase + k, cpeer)
            issue(1)
        for k in range(nz):
            src = zmove(xpeer, -k)
            arrive(src, xbase + k)
            send(src, cbase + nz + k, cpeer)
            issue(1)
        xc = cpeer + 2 - 4 * xbit
        for k in range(nz):
            arrive(zmove(cpeer, -k), cbase + k)
            arrive(zmove(xc, -k), cbase + nz + k)
        return sends

    sends0 = gather(0)
    for s in range(n):
        normed[:, s * shard : (s + 1) * shard] = full[0, s]

    part = jnp.zeros((rows, shard), F32)
    o_copies = w_copies("o")
    for c in range(chunks):
        o_copies[c].wait()
        issue(1)
        part += jnp.dot(
            normed[:, c * kc : (c + 1) * kc], buf_o[c * kc : (c + 1) * kc, :], preferred_element_type=F32
        )
    full[1, me] = part.astype(BF16)
    sends1 = gather(1)
    for s in range(n):
        sl = slice(s * shard, (s + 1) * shard)
        resid[:, sl] = resid[:, sl] + full[1, s].astype(F32)

    def feed(gate_buf, up_buf, names, index):
        norm_into(index)
        g_copies, u_copies = w_copies(names[0]), w_copies(names[1])
        gated = jnp.zeros((rows, hidden_cols), F32)
        lifted = jnp.zeros((rows, hidden_cols), F32)
        for c in range(chunks):
            x = normed[:, c * kc : (c + 1) * kc]
            g_copies[c].wait()
            gated += jnp.dot(x, gate_buf[c * kc : (c + 1) * kc, :hidden_cols], preferred_element_type=F32)
        for c in range(chunks):
            x = normed[:, c * kc : (c + 1) * kc]
            u_copies[c].wait()
            lifted += jnp.dot(x, up_buf[c * kc : (c + 1) * kc, :], preferred_element_type=F32)
        return (gated / (1.0 + jnp.exp(-gated)) * lifted).astype(BF16)

    def down_reduce(hidden, ph):
        sends = []
        for j in range(2 * nz):
            k = j % nz
            xsel = (1 - xbit) if j < nz else xbit
            q = lax.rem(zpos + k, nz) * 2 + xsel
            both = jnp.dot(
                hidden,
                buf_d[:, pl.ds(pl.multiple_of(q * 2 * shard, LANES), 2 * shard)],
                preferred_element_type=F32,
            )
            left, right = both[:, :shard], both[:, shard:]
            is_left = jnp.zeros((rows, shard), jnp.int32) + core == 0
            acc[j] = jnp.where(is_left, left, right)
            cout[ph, j] = jnp.where(is_left, right, left).astype(BF16)
            cp = rcopy(cout.at[ph, j], crecv.at[ph, j], rs_send.at[ph, j], rs_recv.at[ph, j], cpeer)
            cp.start()
            sends.append(cp)
            issue(1)
        if ph == 0:
            pending.extend(w_copies("d2"))
        for k in range(nz):
            sends[k].wait_recv()
            xout[ph, k] = (acc[k] + crecv[ph, k].astype(F32)).astype(BF16)
            cp = rcopy(
                xout.at[ph, k], xrecv.at[ph, k],
                rs_send.at[ph, 2 * nz + k], rs_recv.at[ph, 2 * nz + k], xpeer,
            )
            cp.start()
            sends.append(cp)
            issue(1)
        for k in list(range(1, nz)) + [0]:
            sends[nz + k].wait_recv()
            sends[2 * nz + k].wait_recv()
            val = acc[nz + k] + crecv[ph, nz + k].astype(F32) + xrecv[ph, k].astype(F32)
            if k:
                zout[ph, k] = val.astype(BF16)
                cp = rcopy(
                    zout.at[ph, k], zrecv.at[ph, k],
                    rs_send.at[ph, 3 * nz + k], rs_recv.at[ph, 3 * nz + k], zmove(me, k),
                )
                cp.start()
                sends.append(cp)
            else:
                own[...] = val
        for k in range(1, nz):
            sends[3 * nz + k - 1].wait_recv()
            own[...] = own[...] + zrecv[ph, k].astype(F32)
        return sends

    issue(len(pending))
    hidden = feed(buf_g, buf_u, ("g1", "u1"), 1)
    pending.extend(w_copies("u2"))
    wait_all("d1")
    sends2 = down_reduce(hidden, 0)
    full[2, me] = own[...].astype(BF16)
    sends3 = gather(2)
    for s in range(n):
        sl = slice(s * shard, (s + 1) * shard)
        resid[:, sl] = resid[:, sl] + full[2, s].astype(F32)

    issue(len(pending))
    hidden = feed(buf_a, buf_g, ("g2", "u2"), 2)
    wait_all("d2")
    sends4 = down_reduce(hidden, 1)
    own[...] = own[...] + resid[:, pl.ds(pl.multiple_of(me * shard, LANES), shard)]

    for p in range(pos):
        for m in range(micro):
            for k in range(sub):
                fin[p, m * sub + k : m * sub + k + 1, :] = own[m * pos + p : m * pos + p + 1, k * LANES : (k + 1) * LANES]
    fin_sends = []
    for k in range(1, n):
        dev = lax.rem(me + k, n)
        cp = rcopy(fin.at[dev], finr.at[me], f_send.at[k], f_recv.at[k], dev)
        cp.start()
        fin_sends.append(cp)
    finr[me] = fin[me]
    for k in range(1, n):
        src = lax.rem(me + n - k, n)
        rcopy(fin.at[src], finr.at[src], f_send.at[k], f_recv.at[k], src).wait_recv()
    for s in range(n):
        for m in range(micro):
            for k in range(sub):
                lo = s * shard + k * LANES
                rows_out[m : m + 1, lo : lo + LANES] = finr[s, m * sub + k : m * sub + k + 1, :]
    out_ref[0] = rows_out[...].astype(BF16)

    for cp in tok_sends + sends0 + sends1 + sends2 + sends3 + sends4 + fin_sends:
        cp.wait_send()
    for j in range(nblk):
        owner, slot = block_target(j)

        @pl.when(owner != me)
        def _():
            rcopy(blocks.at[j], qkv.at[slot], q_send.at[j], q_recv.at[slot], owner).wait_send()


def local_fused(n, kc, *args):
    token_ids, lengths, embed_table = args[:3]
    micro = token_ids.shape[1]
    vocab, width = embed_table.shape
    rows = n * micro
    shard = width // n
    hidden_cols = args[7].shape[1]
    nblk = 3 * width // HD // n
    nz = n // 4
    chunks = width // kc
    tall = lambda gain: gain.reshape(1, width)
    operands = list(args)
    for at in (3, 6, 10):
        operands[at] = tall(args[at])
    smem = pl.BlockSpec(memory_space=pltpu.SMEM)
    hbm = pl.BlockSpec(memory_space=pl.ANY)
    dma = pltpu.SemaphoreType.DMA
    weight_bytes = sum(a.size * a.dtype.itemsize for a in args)
    return pl.pallas_call(
        functools.partial(fused_kernel, n, micro, vocab, kc),
        out_shape=jax.ShapeDtypeStruct((1, micro, width), BF16),
        in_specs=[smem, smem] + [hbm] * 12,
        out_specs=pl.BlockSpec(memory_space=pltpu.VMEM),
        scratch_shapes=[
            pltpu.VMEM((width, nblk * HD), BF16),
            pltpu.VMEM((width, shard), BF16),
            pltpu.VMEM((width, hidden_cols), BF16),
            pltpu.VMEM((width, hidden_cols), BF16),
            pltpu.VMEM((hidden_cols, width), BF16),
            pltpu.VMEM((vocab, width), BF16),
            pltpu.VMEM((3, 1, width), F32),
            pltpu.VMEM((n, 8, LANES), jnp.int32),
            pltpu.VMEM((rows, vocab), F32),
            pltpu.VMEM((rows, width), F32),
            pltpu.VMEM((rows, width), BF16),
            pltpu.VMEM((nblk, rows, HD), BF16),
            pltpu.VMEM((nblk, rows, HD), BF16),
            pltpu.VMEM((3, n, rows, shard), BF16),
            pltpu.VMEM((2 * nz, rows, shard), F32),
            pltpu.VMEM((2, 2 * nz, rows, shard), BF16),
            pltpu.VMEM((2, 2 * nz, rows, shard), BF16),
            pltpu.VMEM((2, nz, rows, shard), BF16),
            pltpu.VMEM((2, nz, rows, shard), BF16),
            pltpu.VMEM((2, nz, rows, shard), BF16),
            pltpu.VMEM((2, nz, rows, shard), BF16),
            pltpu.VMEM((rows, shard), F32),
            pltpu.VMEM((n, 8, LANES), F32),
            pltpu.VMEM((n, 8, LANES), F32),
            pltpu.VMEM((micro, width), F32),
            dma((8, max(chunks, 8))),
            dma((4,)),
            dma((n,)),
            dma((n,)),
            dma((nblk,)),
            dma((nblk,)),
            dma((3, n)),
            dma((3, n)),
            dma((2, n)),
            dma((2, n)),
            dma((n,)),
            dma((n,)),
        ],
        compiler_params=pltpu.CompilerParams(
            collective_id=0, has_side_effects=True, vmem_limit_bytes=63 * 1024 * 1024
        ),
        cost_estimate=pl.CostEstimate(
            flops=rows * weight_bytes, bytes_accessed=weight_bytes, transcendentals=0
        ),
    )(*operands)


def local(n, *args):
    token_ids, embed_table = args[0], args[2]
    width, hidden_cols = embed_table.shape[1], args[7].shape[1]
    rows_here, micro = token_ids.shape
    kc = next((k for k in (1024, 512, 256, LANES) if width % k == 0), 0)
    fits = (
        rows_here == 1
        and n % 4 == 0
        and kc > 0
        and width % (n * HD) == 0
        and hidden_cols % LANES == 0
        and hidden_cols <= args[4].shape[1]
        and micro * (width // n // LANES) <= 8
        and (micro * n) % 16 == 0
        and embed_table.shape[0] <= LANES
        and sum(a.size * a.dtype.itemsize for a in args) <= 100 * 1024 * 1024
    )
    return local_fused(n, kc, *args) if fits else local_general(*args)


def solution(mesh):
    return jax.shard_map(
        functools.partial(local, mesh.shape["tensor"]),
        mesh=mesh,
        in_specs=(
            P("tensor", "groups"),
            P("groups"),
            P(),
            P(),
            P(None, "tensor"),
            P(None, "tensor"),
            P(),
            P(None, "tensor"),
            P(None, "tensor"),
            P("tensor", None),
            P(),
            P(None, "tensor"),
            P(None, "tensor"),
            P("tensor", None),
        ),
        out_specs=P("tensor", "groups", None),
        check_vma=False,
    )
```

```python
import functools

import jax
import jax.numpy as jnp
from jax import lax
from jax.experimental import pallas as pl
from jax.experimental.pallas import tpu as pltpu
from jax.sharding import PartitionSpec as P

HD = 128
LANES = 128
MESH = pl.DeviceIdType.MESH
F32 = jnp.float32
BF16 = jnp.bfloat16


def norm_rows(values, gain_vec):
    row_mean = jnp.mean(values, axis=-1, keepdims=True)
    centred = values - row_mean
    row_var = jnp.mean(centred * centred, axis=-1, keepdims=True)
    return (centred * lax.rsqrt(row_var + 1e-05) * gain_vec).astype(jnp.bfloat16)


def local_hidden(normed, gate_mat, up_mat):
    gated = jnp.einsum("pmd,dc->pmc", normed, gate_mat, preferred_element_type=jnp.float32)
    lifted = jnp.einsum("pmd,dc->pmc", normed, up_mat, preferred_element_type=jnp.float32)
    return (jax.nn.silu(gated) * lifted).astype(jnp.bfloat16)


def spread_rows(local_rows, row_fn):
    return row_fn(lax.all_gather(local_rows, "tensor", axis=0, tiled=True))


def to_tokens(columns):
    return lax.all_to_all(columns, "tensor", split_axis=0, concat_axis=2, tiled=True)


def local_general(
    token_ids, lengths, embed_table, gain_attn, w_qkv, w_out,
    gain_first, gate_first, up_first, down_first,
    gain_second, gate_second, up_second, down_second,
):
    rows_here, micro_count = token_ids.shape
    vocab_size, width = embed_table.shape
    heads = width // HD
    own_start = lax.axis_index("tensor") * rows_here
    onehot = (token_ids[:, :, None] == jnp.arange(vocab_size)[None, None, :]).astype(jnp.bfloat16)
    embedded = jnp.einsum("pmv,vd->pmd", onehot, embed_table, preferred_element_type=jnp.float32)

    def matmul_rows(weight):
        return lambda rows: jnp.einsum(
            "pmd,dc->pmc", rows, weight, preferred_element_type=jnp.float32
        ).astype(jnp.bfloat16)

    projected = to_tokens(spread_rows(norm_rows(embedded, gain_attn), matmul_rows(w_qkv)))
    queries = projected[..., :width].reshape(rows_here, micro_count, heads, HD)
    keys = lax.all_gather(projected[..., width : 2 * width], "tensor", axis=0, tiled=True)
    values = lax.all_gather(projected[..., 2 * width :], "tensor", axis=0, tiled=True)
    total = keys.shape[0]
    keys = keys.reshape(total, micro_count, heads, HD)
    values = values.reshape(total, micro_count, heads, HD)
    scores = jnp.einsum("pmhe,qmhe->pmhq", queries, keys, preferred_element_type=jnp.float32)
    live = (jnp.arange(total)[None, :] < lengths[:, None]).astype(jnp.float32)
    weights = jnp.exp(scores * HD ** (-0.5)) * live[None, :, None, :]
    numerator = jnp.einsum(
        "pmhq,qmhe->pmhe", weights.astype(jnp.bfloat16), values, preferred_element_type=jnp.float32
    )
    attended = numerator / jnp.sum(weights, axis=-1)[..., None]
    attended = attended.reshape(rows_here, micro_count, width).astype(jnp.bfloat16)
    after_attn = embedded + to_tokens(spread_rows(attended, matmul_rows(w_out))).astype(jnp.float32)
    hidden_first = spread_rows(
        norm_rows(after_attn, gain_first), lambda rows: local_hidden(rows, gate_first, up_first)
    )
    partial_all = jnp.einsum(
        "pmc,cd->pmd", hidden_first, down_first, preferred_element_type=jnp.float32
    )
    own_rows = lax.dynamic_slice_in_dim(partial_all, own_start, rows_here, 0) + after_attn
    partial_all = lax.dynamic_update_slice_in_dim(partial_all, own_rows, own_start, 0)
    first_all = lax.psum(partial_all, "tensor")
    after_first = lax.dynamic_slice_in_dim(first_all, own_start, rows_here, 0)
    hidden_second = local_hidden(norm_rows(first_all, gain_second), gate_second, up_second)
    second = jnp.einsum(
        "pmc,cd->pmd", hidden_second, down_second, preferred_element_type=jnp.float32
    )
    after_second = after_first + lax.psum_scatter(
        second, "tensor", scatter_dimension=0, tiled=True
    )
    return after_second.astype(jnp.bfloat16)


def fused_kernel(
    n, micro, vocab, kc,
    tok_ref, len_ref, emb_hbm, ga_hbm, wq_hbm, wo_hbm,
    gf_hbm, g1_hbm, u1_hbm, d1_hbm, gs_hbm, g2_hbm, u2_hbm, d2_hbm,
    out_ref,
    buf_a, buf_o, buf_g, buf_u, buf_d,
    emb_ref, gain_ref,
    toks, onehot, resid, normed, blocks, qkv, full, acc, cout, crecv, xout, xrecv, zout, zrecv,
    own, fin, finr, rows_out, oacc, gacc, uacc, stat,
    w_sem, e_sem, small_send, small_recv, q_send, q_recv, ag_send, ag_recv,
    rs_send, rs_recv, f_send, f_recv,
):
    width = emb_ref.shape[1]
    pos = n
    rows = micro * pos
    shard = width // n
    hidden_cols = buf_g.shape[1]
    hpd = width // HD // n
    nblk = 3 * hpd
    heads = width // HD
    nz = n // 4
    chunks = width // kc
    sub = shard // LANES

    me = lax.axis_index("tensor")
    grp = lax.axis_index("groups")
    core = lax.rem(me, 2)
    xbit = lax.rem(me // 2, 2)
    zpos = me // 4
    cpeer = me + 1 - 2 * core
    xpeer = me + 2 - 4 * xbit

    def zmove(dev, k):
        return lax.rem(dev + 4 * k + n, n)

    def rcopy(src, dst, ssem, rsem, dev):
        return pltpu.make_async_remote_copy(
            src_ref=src, dst_ref=dst, send_sem=ssem, recv_sem=rsem,
            device_id=(grp, dev), device_id_type=MESH,
        )

    def row_chunk(ref, c):
        return ref.at[pl.ds(c * kc, kc)]

    dparts = 8
    dk = hidden_cols // dparts

    def w_copies(which):
        if which == "q":
            return [pltpu.make_async_copy(row_chunk(wq_hbm, c), row_chunk(buf_a, c), w_sem.at[0, c]) for c in range(chunks)]
        if which == "o":
            return [pltpu.make_async_copy(row_chunk(wo_hbm, c), row_chunk(buf_o, c), w_sem.at[1, c]) for c in range(chunks)]
        if which == "g1":
            return [pltpu.make_async_copy(row_chunk(g1_hbm, c), row_chunk(buf_g, c), w_sem.at[2, c]) for c in range(chunks)]
        if which == "u1":
            return [pltpu.make_async_copy(row_chunk(u1_hbm, c), row_chunk(buf_u, c), w_sem.at[3, c]) for c in range(chunks)]
        if which == "g2":
            return [
                pltpu.make_async_copy(
                    row_chunk(g2_hbm, c), buf_a.at[pl.ds(c * kc, kc), pl.ds(0, hidden_cols)], w_sem.at[4, c]
                )
                for c in range(chunks)
            ]
        if which == "u2":
            return [pltpu.make_async_copy(row_chunk(u2_hbm, c), row_chunk(buf_g, c), w_sem.at[5, c]) for c in range(chunks)]
        src = d1_hbm if which == "d1" else d2_hbm
        row = 6 if which == "d1" else 7
        return [
            pltpu.make_async_copy(src.at[pl.ds(c * dk, dk)], buf_d.at[pl.ds(c * dk, dk)], w_sem.at[row, c])
            for c in range(dparts)
        ]

    pending = []

    def issue(count):
        for cp in pending[:count]:
            cp.start()
        del pending[:count]

    def wait_all(which):
        for cp in w_copies(which):
            cp.wait()

    small = [
        pltpu.make_async_copy(emb_hbm, emb_ref, e_sem.at[0]),
        pltpu.make_async_copy(ga_hbm, gain_ref.at[0], e_sem.at[1]),
        pltpu.make_async_copy(gf_hbm, gain_ref.at[1], e_sem.at[2]),
        pltpu.make_async_copy(gs_hbm, gain_ref.at[2], e_sem.at[3]),
    ]
    for cp in small:
        cp.start()
    pending.extend(w_copies("q") + w_copies("o") + w_copies("g1") + w_copies("u1") + w_copies("d1"))
    issue(chunks // 2)

    tile_row = lax.broadcasted_iota(jnp.int32, (8, LANES), 0)
    tile = jnp.zeros((8, LANES), jnp.int32)
    for m in range(micro):
        tile = jnp.where(tile_row == m, tok_ref[0, m], tile)
    toks[me] = tile

    barrier = pltpu.get_barrier_semaphore()
    for k in range(1, n):
        pl.semaphore_signal(barrier, inc=1, device_id=(grp, lax.rem(me + k, n)), device_id_type=MESH)
    pl.semaphore_wait(barrier, n - 1)

    tok_sends = [
        rcopy(toks.at[me], toks.at[me], small_send.at[k], small_recv.at[k], lax.rem(me + k, n))
        for k in range(1, n)
    ]
    for cp in tok_sends:
        cp.start()
    issue(chunks - chunks // 2)
    for k in range(1, n):
        src = lax.rem(me + n - k, n)
        rcopy(toks.at[src], toks.at[src], small_send.at[k], small_recv.at[k], src).wait_recv()

    lane = lax.broadcasted_iota(jnp.int32, (1, vocab), 1)
    for p in range(pos):
        for m in range(micro):
            onehot[m * pos + p : m * pos + p + 1, :] = (toks[p, m : m + 1, :vocab] == lane).astype(F32)
    for cp in small:
        cp.wait()
    hot = onehot[...].astype(BF16)
    for c in range(chunks):
        sl = slice(c * kc, (c + 1) * kc)
        resid[:, sl] = jnp.dot(hot, emb_ref[:, sl], preferred_element_type=F32)

    def norm_into(index):
        total = jnp.zeros((rows, 1), F32)
        for c in range(chunks):
            total += jnp.sum(resid[:, c * kc : (c + 1) * kc], axis=1, keepdims=True)
        mean = total * (1.0 / width)
        var = jnp.zeros((rows, 1), F32)
        for c in range(chunks):
            cen = resid[:, c * kc : (c + 1) * kc] - mean
            var += jnp.sum(cen * cen, axis=1, keepdims=True)
        inv = lax.rsqrt(var * (1.0 / width) + 1e-05)
        for c in range(chunks):
            sl = slice(c * kc, (c + 1) * kc)
            normed[:, sl] = ((resid[:, sl] - mean) * inv * gain_ref[index, :, sl]).astype(BF16)
        return mean

    mean0 = norm_into(0)

    part = jnp.zeros((rows, nblk * HD), F32)
    q_copies = w_copies("q")
    for c in range(chunks):
        q_copies[c].wait()
        part += jnp.dot(
            normed[:, c * kc : (c + 1) * kc], buf_a[c * kc : (c + 1) * kc, :], preferred_element_type=F32
        )
    for j in range(nblk):
        blocks[j] = part[:, j * HD : (j + 1) * HD].astype(BF16)

    def block_target(j):
        g = me * nblk + j
        kind = g // heads
        head = lax.rem(g, heads)
        return head // hpd, kind * hpd + lax.rem(head, hpd)

    for j in range(nblk):
        owner, slot = block_target(j)

        @pl.when(owner != me)
        def _():
            rcopy(blocks.at[j], qkv.at[slot], q_send.at[j], q_recv.at[slot], owner).start()

        @pl.when(owner == me)
        def _():
            pltpu.make_async_copy(blocks.at[j], qkv.at[slot], q_recv.at[slot]).start()

    pending.extend(w_copies("g2"))
    issue(3 * chunks)

    for slot in range(nblk):
        pltpu.make_async_copy(blocks.at[0], qkv.at[slot], q_recv.at[slot]).wait()

    ri = lax.broadcasted_iota(jnp.int32, (rows, rows), 0)
    ci = lax.broadcasted_iota(jnp.int32, (rows, rows), 1)
    live = jnp.zeros((rows, rows), F32)
    for m in range(micro):
        inside = (ri >= m * pos) & (ri < (m + 1) * pos) & (ci >= m * pos) & (ci < m * pos + len_ref[m])
        live = jnp.where(inside, 1.0, live)
    for h in range(hpd):
        scores = lax.dot_general(
            qkv[h], qkv[hpd + h], (((1,), (1,)), ((), ())), preferred_element_type=F32
        ) * (HD ** (-0.5))
        weights = jnp.where(live > 0.5, jnp.exp(scores), 0.0)
        denominator = jnp.sum(weights, axis=1, keepdims=True)
        numerator = jnp.dot(weights.astype(BF16), qkv[2 * hpd + h], preferred_element_type=F32)
        full[0, me, :, h * HD : (h + 1) * HD] = (numerator / denominator).astype(BF16)

    def gather(ph, work):
        buf = full.at[ph]
        sends = []

        def send(slot, idx, dev):
            cp = rcopy(buf.at[slot], buf.at[slot], ag_send.at[ph, idx], ag_recv.at[ph, idx], dev)
            cp.start()
            sends.append(cp)

        def arrive(slot, idx):
            rcopy(buf.at[slot], buf.at[slot], ag_send.at[ph, idx], ag_recv.at[ph, idx], cpeer).wait_recv()

        xbase, cbase = nz, 2 * nz
        for k in range(1, nz):
            send(me, k, zmove(me, k))
        send(me, xbase, xpeer)
        send(me, cbase, cpeer)
        issue(1)
        arrive(cpeer, cbase)
        work(me // 2)
        for k in range(1, nz):
            src = zmove(me, -k)
            arrive(src, k)
            send(src, xbase + k, xpeer)
            send(src, cbase + k, cpeer)
            issue(1)

        def forward(k):
            src = zmove(xpeer, -k)
            arrive(src, xbase + k)
            send(src, cbase + nz + k, cpeer)
            issue(1)

        xc = cpeer + 2 - 4 * xbit
        for k in range(1, nz):
            arrive(zmove(cpeer, -k), cbase + k)
            work(zmove(me, -k) // 2)
            forward(k - 1)
        forward(nz - 1)
        for k in range(nz):
            arrive(zmove(xc, -k), cbase + nz + k)
            work(zmove(xpeer, -k) // 2)
        return sends

    def pair_of(ph, q):
        return jnp.concatenate([full[ph, 2 * q], full[ph, 2 * q + 1]], axis=1)

    def pair_span(q):
        return pl.ds(pl.multiple_of(q * 2 * shard, LANES), 2 * shard)

    wait_all("o")
    oacc[...] = jnp.zeros_like(oacc)

    def out_work(q):
        oacc[...] += jnp.dot(pair_of(0, q), buf_o[pair_span(q), :], preferred_element_type=F32)

    sends0 = gather(0, out_work)
    full[1, me] = oacc[...].astype(BF16)
    def feed(ph, gate_buf, up_buf, index, mean_before):
        gacc[...] = jnp.zeros_like(gacc)
        uacc[...] = jnp.zeros_like(uacc)
        stat[...] = jnp.zeros_like(stat)

        def work(q):
            span = pair_span(q)
            x = resid[:, span] + pair_of(ph, q).astype(F32)
            resid[:, span] = x
            cen = x - mean_before
            stat[0] += jnp.sum(cen, axis=1, keepdims=True)
            stat[1] += jnp.sum(cen * cen, axis=1, keepdims=True)
            gain = gain_ref[index, :, span]
            lhs = jnp.concatenate([cen * gain, jnp.broadcast_to(gain, (16, 2 * shard))], axis=0).astype(BF16)
            gacc[...] += jnp.dot(lhs, gate_buf[span, :hidden_cols], preferred_element_type=F32)
            uacc[...] += jnp.dot(lhs, up_buf[span, :], preferred_element_type=F32)

        sends = gather(ph, work)
        shift = stat[0] * (1.0 / width)
        inv = lax.rsqrt(stat[1] * (1.0 / width) - shift * shift + 1e-05)
        gated = inv * (gacc[:rows, :] - shift * gacc[rows : rows + 1, :])
        lifted = inv * (uacc[:rows, :] - shift * uacc[rows : rows + 1, :])
        hidden = (gated / (1.0 + jnp.exp(-gated)) * lifted).astype(BF16)
        return hidden, mean_before + shift, sends

    def down_reduce(hidden, ph):
        sends = {}

        def send(idx, src, dst, dev):
            cp = rcopy(src, dst, rs_send.at[ph, idx], rs_recv.at[ph, idx], dev)
            cp.start()
            sends[idx] = cp

        def column_sum(j):
            k = j % nz
            xsel = (1 - xbit) if j < nz else xbit
            q = lax.rem(zpos + k, nz) * 2 + xsel
            both = jnp.dot(hidden, buf_d[:, pair_span(q)], preferred_element_type=F32)
            left, right = both[:, :shard], both[:, shard:]
            is_left = jnp.zeros((rows, shard), jnp.int32) + core == 0
            acc[j] = jnp.where(is_left, left, right)
            cout[ph, j] = jnp.where(is_left, right, left).astype(BF16)
            send(j, cout.at[ph, j], crecv.at[ph, j], cpeer)

        def along_x(k):
            sends[k].wait_recv()
            xout[ph, k] = (acc[k] + crecv[ph, k].astype(F32)).astype(BF16)
            send(2 * nz + k, xout.at[ph, k], xrecv.at[ph, k], xpeer)

        def along_z(k):
            sends[nz + k].wait_recv()
            sends[2 * nz + k].wait_recv()
            val = acc[nz + k] + crecv[ph, nz + k].astype(F32) + xrecv[ph, k].astype(F32)
            if k:
                zout[ph, k] = val.astype(BF16)
                send(3 * nz + k, zout.at[ph, k], zrecv.at[ph, k], zmove(me, k))
            else:
                own[...] = val

        order = list(range(1, nz)) + [0]
        for k in order:
            column_sum(k)
            issue(1)
        for t, k in enumerate(order):
            column_sum(nz + k)
            issue(1)
            along_x(k)
            if t >= 2:
                along_z(order[t - 2])
        if ph == 0:
            pending.extend(w_copies("d2"))
        for k in order[max(nz - 2, 0) :]:
            along_z(k)
        for k in range(1, nz):
            sends[3 * nz + k].wait_recv()
            own[...] = own[...] + zrecv[ph, k].astype(F32)
        return list(sends.values())

    wait_all("g1")
    wait_all("u1")
    hidden, mean1, sends1 = feed(1, buf_g, buf_u, 1, mean0)
    issue(len(pending))
    pending.extend(w_copies("u2"))
    issue(2)
    wait_all("d1")
    sends2 = down_reduce(hidden, 0)
    issue(2)
    full[2, me] = own[...].astype(BF16)
    wait_all("g2")
    wait_all("u2")
    hidden, _, sends3 = feed(2, buf_a, buf_g, 2, mean1)
    issue(len(pending))
    wait_all("d2")
    sends4 = down_reduce(hidden, 1)
    own[...] = own[...] + resid[:, pl.ds(pl.multiple_of(me * shard, LANES), shard)]

    for p in range(pos):
        for m in range(micro):
            for k in range(sub):
                fin[p, m * sub + k : m * sub + k + 1, :] = own[m * pos + p : m * pos + p + 1, k * LANES : (k + 1) * LANES]
    fin_sends = []
    for k in range(1, n):
        dev = lax.rem(me + k, n)
        cp = rcopy(fin.at[dev], finr.at[me], f_send.at[k], f_recv.at[k], dev)
        cp.start()
        fin_sends.append(cp)
    finr[me] = fin[me]
    for k in range(1, n):
        src = lax.rem(me + n - k, n)
        rcopy(fin.at[src], finr.at[src], f_send.at[k], f_recv.at[k], src).wait_recv()
    for s in range(n):
        for m in range(micro):
            for k in range(sub):
                lo = s * shard + k * LANES
                rows_out[m : m + 1, lo : lo + LANES] = finr[s, m * sub + k : m * sub + k + 1, :]
    out_ref[0] = rows_out[...].astype(BF16)

    for cp in tok_sends + sends0 + sends1 + sends2 + sends3 + sends4 + fin_sends:
        cp.wait_send()
    for j in range(nblk):
        owner, slot = block_target(j)

        @pl.when(owner != me)
        def _():
            rcopy(blocks.at[j], qkv.at[slot], q_send.at[j], q_recv.at[slot], owner).wait_send()


def local_fused(n, kc, *args):
    token_ids, lengths, embed_table = args[:3]
    micro = token_ids.shape[1]
    vocab, width = embed_table.shape
    rows = n * micro
    shard = width // n
    hidden_cols = args[7].shape[1]
    nblk = 3 * width // HD // n
    nz = n // 4
    chunks = width // kc
    tall = lambda gain: gain.reshape(1, width)
    operands = list(args)
    for at in (3, 6, 10):
        operands[at] = tall(args[at])
    smem = pl.BlockSpec(memory_space=pltpu.SMEM)
    hbm = pl.BlockSpec(memory_space=pl.ANY)
    dma = pltpu.SemaphoreType.DMA
    weight_bytes = sum(a.size * a.dtype.itemsize for a in args)
    return pl.pallas_call(
        functools.partial(fused_kernel, n, micro, vocab, kc),
        out_shape=jax.ShapeDtypeStruct((1, micro, width), BF16),
        in_specs=[smem, smem] + [hbm] * 12,
        out_specs=pl.BlockSpec(memory_space=pltpu.VMEM),
        scratch_shapes=[
            pltpu.VMEM((width, nblk * HD), BF16),
            pltpu.VMEM((width, shard), BF16),
            pltpu.VMEM((width, hidden_cols), BF16),
            pltpu.VMEM((width, hidden_cols), BF16),
            pltpu.VMEM((hidden_cols, width), BF16),
            pltpu.VMEM((vocab, width), BF16),
            pltpu.VMEM((3, 1, width), F32),
            pltpu.VMEM((n, 8, LANES), jnp.int32),
            pltpu.VMEM((rows, vocab), F32),
            pltpu.VMEM((rows, width), F32),
            pltpu.VMEM((rows, width), BF16),
            pltpu.VMEM((nblk, rows, HD), BF16),
            pltpu.VMEM((nblk, rows, HD), BF16),
            pltpu.VMEM((3, n, rows, shard), BF16),
            pltpu.VMEM((2 * nz, rows, shard), F32),
            pltpu.VMEM((2, 2 * nz, rows, shard), BF16),
            pltpu.VMEM((2, 2 * nz, rows, shard), BF16),
            pltpu.VMEM((2, nz, rows, shard), BF16),
            pltpu.VMEM((2, nz, rows, shard), BF16),
            pltpu.VMEM((2, nz, rows, shard), BF16),
            pltpu.VMEM((2, nz, rows, shard), BF16),
            pltpu.VMEM((rows, shard), F32),
            pltpu.VMEM((n, 8, LANES), F32),
            pltpu.VMEM((n, 8, LANES), F32),
            pltpu.VMEM((micro, width), F32),
            pltpu.VMEM((rows, shard), F32),
            pltpu.VMEM((rows + 16, hidden_cols), F32),
            pltpu.VMEM((rows + 16, hidden_cols), F32),
            pltpu.VMEM((2, rows, 1), F32),
            dma((8, max(chunks, 8))),
            dma((4,)),
            dma((n,)),
            dma((n,)),
            dma((nblk,)),
            dma((nblk,)),
            dma((3, n)),
            dma((3, n)),
            dma((2, n)),
            dma((2, n)),
            dma((n,)),
            dma((n,)),
        ],
        compiler_params=pltpu.CompilerParams(
            collective_id=0, has_side_effects=True, vmem_limit_bytes=63 * 1024 * 1024
        ),
        cost_estimate=pl.CostEstimate(
            flops=rows * weight_bytes, bytes_accessed=weight_bytes, transcendentals=0
        ),
    )(*operands)


def local(n, *args):
    token_ids, embed_table = args[0], args[2]
    width, hidden_cols = embed_table.shape[1], args[7].shape[1]
    rows_here, micro = token_ids.shape
    kc = next((k for k in (1024, 512, 256, LANES) if width % k == 0), 0)
    fits = (
        rows_here == 1
        and n % 4 == 0
        and kc > 0
        and width % (n * HD) == 0
        and hidden_cols % LANES == 0
        and hidden_cols <= args[4].shape[1]
        and micro * (width // n // LANES) <= 8
        and (micro * n) % 16 == 0
        and embed_table.shape[0] <= LANES
        and sum(a.size * a.dtype.itemsize for a in args) <= 100 * 1024 * 1024
    )
    return local_fused(n, kc, *args) if fits else local_general(*args)


def solution(mesh):
    return jax.shard_map(
        functools.partial(local, mesh.shape["tensor"]),
        mesh=mesh,
        in_specs=(
            P("tensor", "groups"),
            P("groups"),
            P(),
            P(),
            P(None, "tensor"),
            P(None, "tensor"),
            P(),
            P(None, "tensor"),
            P(None, "tensor"),
            P("tensor", None),
            P(),
            P(None, "tensor"),
            P(None, "tensor"),
            P("tensor", None),
        ),
        out_specs=P("tensor", "groups", None),
        check_vma=False,
    )
```
